256 devices in a mesh: prow: 4 (over y), pcol: 64 (over z, x, core).
Axes of the slice: x: 4, y: 4, z: 8, core: 2. Of those that a mesh axis runs over, the one named last changes fastest.
Arguments:
- rhs: bfloat16 [12, 4096, 384], P(None, ('prow', 'pcol')), may hold values from -6 to 6
- factor_blocks: bfloat16 [48, 4, 64, 16, 4096], P(None, None, 'pcol', None, 'prow'), may hold values from -0.046875 to 0.046875
- diag_inverses: bfloat16 [12, 4, 64, 16, 4096], P(None, None, 'pcol', None, 'prow'), as said below
- block_index: int32 [48, 2], replicated, may hold values from 0 to 11, as said below
Outputs:
- solution: bfloat16 [12, 4096, 384], P(None, ('prow', 'pcol'))
The draws below stay inside these ranges and needn't reach their ends.
Inputs may be any that keep to these rules, and one draw needn't show every extreme that they name: `block_index`: 48 distinct pairs (block row, block column) with column < row, listed by row and then by column. `diag_inverses`: each D_j is lower triangular (zero above the diagonal) with a positive diagonal between 0.5 and 1.
All inputs are finite; a program needn't handle non-finite values.
Results may differ from the reference program's by a relative error of at most 0.013.
Values may be sent and summed in bfloat16 or wider, within the bound.
No kernel may reach another device: no remote copies, remote signals or barrier semaphores. Data moves between devices by JAX's collectives and lax.ppermute only.
A program may use at most 64 MiB of HBM per device.

```python
import jax
import jax.numpy as jnp
import numpy as np
from jax import lax

BS = 4096
NRHS = 384
NB = 12
NNZ = 48
PROWS = 4
PCOLS = 64
SUB = 16


def draw_diag_inverses(key, part):
    key = jax.random.fold_in(key, 11)
    key_off, key_diag = jax.random.split(key)
    spread = 0.4 * 2.0 ** 0.5 * BS ** (-0.5)
    off_diag = jax.random.normal(key_off, (NB, BS, BS), jnp.float32) * spread
    diagonal = jax.random.uniform(key_diag, (NB, BS, 1), jnp.float32, 0.5, 1.0)
    row_ids = jnp.arange(BS)[:, None]
    col_ids = jnp.arange(BS)[None, :]
    unit = (row_ids == col_ids).astype(jnp.float32)
    below = (row_ids > col_ids).astype(jnp.float32)
    full = off_diag * below + diagonal * unit
    return full.reshape(NB, PROWS, PCOLS, SUB, BS).astype(jnp.bfloat16)


def draw_block_index(key, part):
    key = jax.random.fold_in(key, 23)
    lower_rows, lower_cols = np.tril_indices(NB, -1)
    picked = jax.random.permutation(key, lower_rows.shape[0])[:NNZ]
    chosen = jnp.sort(picked)
    rows_taken = jnp.asarray(lower_rows, jnp.int32)[chosen]
    cols_taken = jnp.asarray(lower_cols, jnp.int32)[chosen]
    return jnp.stack([rows_taken, cols_taken], axis=1).astype(jnp.int32)


def block_levels(key, extent, cuts, low, high):
    level = 1.0
    for axis_at, blocks in cuts:
        heights = jax.random.uniform(jax.random.fold_in(jax.random.fold_in(key, 6), axis_at), (blocks,), jnp.float32, low / len(cuts), high / len(cuts))
        level = level * jnp.repeat(jnp.exp(heights), extent[axis_at] // blocks).reshape((-1,) + (1,) * (len(extent) - 1 - axis_at))
    return level


def noise(stream_key, shape, width, most, shards=(), kind=jnp.bfloat16):
    loudness = block_levels(stream_key, shape, shards, -0.22, 0.18) if shards else 1.0
    values = jax.random.normal(stream_key, shape, jnp.float32) * width * loudness
    return jnp.minimum(jnp.maximum(values, -most), most).astype(kind)


def setup_inputs(seed: int = 0) -> dict:
    arg_keys = jax.random.split(jax.random.key(seed), 5)
    return {
        "rhs": noise(arg_keys[0], (NB, BS, NRHS), 1.0, 6.0, ((1, 256),)),
        "factor_blocks": noise(arg_keys[1], (NNZ, PROWS, PCOLS, SUB, BS), (4 * BS) ** -0.5, 0.046875, ((2, 64), (4, 4))),
        "diag_inverses": draw_diag_inverses(jax.random.fold_in(arg_keys[4], 71), 0),
        "block_index": draw_block_index(jax.random.fold_in(arg_keys[4], 71), 0),
    }


def reference(rhs, factor_blocks, diag_inverses, block_index):
    factor = factor_blocks.reshape(NNZ, BS, BS)
    inverse = diag_inverses.reshape(NB, BS, BS)
    block_rows = block_index[:, 0]
    block_cols = block_index[:, 1]
    solution = jnp.zeros((NB, BS, NRHS), jnp.bfloat16)
    for current in range(NB):
        begin = jnp.sum((block_rows < current).astype(jnp.int32)).astype(jnp.int32)
        finish = jnp.sum((block_rows <= current).astype(jnp.int32)).astype(jnp.int32)
        known = solution

        def accumulate(entry, running):
            source = lax.dynamic_index_in_dim(known, block_cols[entry], 0, keepdims=False)
            matrix = lax.dynamic_index_in_dim(factor, entry, 0, keepdims=False)
            return running + jnp.dot(matrix, source, preferred_element_type=jnp.float32)

        update = lax.fori_loop(begin, finish, accumulate, jnp.zeros((BS, NRHS), jnp.float32))
        residual = (rhs[current].astype(jnp.float32) - update).astype(jnp.bfloat16)
        solved = jnp.dot(inverse[current], residual, preferred_element_type=jnp.float32).astype(jnp.bfloat16)
        solution = solution.at[current].set(solved)
    return solution
```

```python
import jax
import jax.numpy as jnp
from jax import lax
from jax.experimental import pallas as pl
from jax.experimental.pallas import tpu as pltpu
from jax.sharding import Mesh, PartitionSpec as P

ROWS, CHIPS, CORES = "prow", "chip", "core"


def spread(copies):
    received = lax.all_to_all(copies, CHIPS, 0, 0, tiled=True)
    return lax.all_gather(received, CORES, axis=0)


def interleave(gathered, whole):
    cores, chips, rows, _ = gathered.shape
    parts = whole.shape[0] // (cores * chips * 16)
    span = cores * chips * 16

    def place(chip, carry):
        for core in range(cores):
            for part in range(parts):
                first = pl.multiple_of(part * span + (chip * cores + core) * 16, 16)
                whole[pl.ds(first, 16), :] = gathered[core, chip, pl.ds(part * 16, 16), :]
        return carry

    lax.fori_loop(0, chips, place, 0, unroll=4)


def product(matrix, whole):
    span = matrix.shape[-1]
    total = None
    for part in range(matrix.shape[0]):
        term = jnp.dot(
            matrix[part], whole[pl.ds(part * span, span), :], preferred_element_type=jnp.float32
        )
        total = term if total is None else total + term
    return total


def copy_out(value, copies):
    for chip in range(copies.shape[0]):
        copies[chip] = value


def solve_kernel(gathered, inverse, copies, piece, whole, matrix, sem):
    load = pltpu.make_async_copy(inverse, matrix, sem)
    load.start()
    interleave(gathered, whole)
    load.wait()
    value = product(matrix, whole).astype(jnp.bfloat16)
    piece[...] = value
    copy_out(value, copies)


def residual_kernel(slots, gathered, factor, rhs, earlier, copies, whole, matrix, total, sem):
    last = slots.shape[0] - 1
    slot = slots[last]

    @pl.when(slot >= 0)
    def _():
        pltpu.make_async_copy(factor.at[:, slot], matrix, sem).start()

    interleave(gathered, whole)
    total[...] = earlier[...]

    @pl.when(slot >= 0)
    def _():
        pltpu.make_async_copy(factor.at[:, slot], matrix, sem).wait()
        total[...] += product(matrix, whole)

    copy_out((rhs[...].astype(jnp.float32) - total[...]).astype(jnp.bfloat16), copies)


def update_kernel(slots, factor, *refs):
    count = len(refs) - 5
    sources = refs[:count]
    total, wholes, matrices, sems, factor_sems = refs[count:]
    for column in range(count):

        @pl.when(slots[column] >= 0)
        def _(column=column):
            pltpu.make_async_copy(
                factor.at[:, slots[column]], matrices.at[column], factor_sems.at[column]
            ).start()
            pltpu.make_async_copy(sources[column], wholes.at[column], sems.at[column]).start()

    total[...] = jnp.zeros_like(total)

    def add(column, carry):
        slot = slots[column]

        @pl.when(slot >= 0)
        def _():
            pltpu.make_async_copy(
                factor.at[:, slot], matrices.at[column], factor_sems.at[column]
            ).wait()
            pltpu.make_async_copy(sources[0], wholes.at[column], sems.at[column]).wait()
            total[...] += product(matrices.at[column], wholes.at[column])

        return carry

    lax.fori_loop(0, count, add, 0)


def vmem():
    return pl.BlockSpec(memory_space=pltpu.VMEM)


def smem():
    return pl.BlockSpec(memory_space=pltpu.SMEM)


def anywhere():
    return pl.BlockSpec(memory_space=pl.ANY)


LIMIT = pltpu.CompilerParams(vmem_limit_bytes=32 * 1024 * 1024)


def solve(gathered, inverse):
    cores, chips, rows, columns = gathered.shape
    parts, _, span = inverse.shape
    return pl.pallas_call(
        solve_kernel,
        out_shape=(
            jax.ShapeDtypeStruct((chips, rows, columns), jnp.bfloat16),
            jax.ShapeDtypeStruct((rows, columns), jnp.bfloat16),
        ),
        in_specs=[vmem(), anywhere()],
        out_specs=(vmem(), vmem()),
        scratch_shapes=[
            pltpu.VMEM((parts * span, columns), jnp.bfloat16),
            pltpu.VMEM(inverse.shape, jnp.bfloat16),
            pltpu.SemaphoreType.DMA,
        ],
        compiler_params=LIMIT,
        name="solve",
    )(gathered, inverse)


def residual(slots, gathered, factor, rhs, earlier):
    cores, chips, rows, columns = gathered.shape
    parts, _, _, span = factor.shape
    return pl.pallas_call(
        residual_kernel,
        out_shape=(
            jax.ShapeDtypeStruct((chips, rows, columns), jnp.bfloat16),
            jax.ShapeDtypeStruct((parts * span, columns), jnp.bfloat16),
        ),
        in_specs=[smem(), vmem(), anywhere(), vmem(), vmem()],
        out_specs=(vmem(), vmem()),
        scratch_shapes=[
            pltpu.VMEM((parts, rows, span), jnp.bfloat16),
            pltpu.VMEM((rows, columns), jnp.float32),
            pltpu.SemaphoreType.DMA,
        ],
        compiler_params=LIMIT,
        name="residual",
    )(slots, gathered, factor, rhs, earlier)


def update(slots, factor, sources):
    parts, _, rows, span = factor.shape
    count = len(sources)
    columns = sources[0].shape[1]
    return pl.pallas_call(
        update_kernel,
        out_shape=jax.ShapeDtypeStruct((rows, columns), jnp.float32),
        in_specs=[smem(), anywhere()] + [anywhere()] * count,
        out_specs=vmem(),
        scratch_shapes=[
            pltpu.VMEM((count, parts * span, columns), jnp.bfloat16),
            pltpu.VMEM((count, parts, rows, span), jnp.bfloat16),
            pltpu.SemaphoreType.DMA((count,)),
            pltpu.SemaphoreType.DMA((count,)),
        ],
        compiler_params=LIMIT,
        cost_estimate=pl.CostEstimate(
            flops=count * 2 * rows * parts * span * 256,
            bytes_accessed=count * parts * span * (rows + 128) * 2,
            transcendentals=0,
        ),
        name="update",
    )(slots, factor, *sources)


def shards(rhs, factor_blocks, diag_inverses, block_index):
    blocks, piece_rows, total_columns = rhs.shape
    entries, parts = factor_blocks.shape[:2]
    span = factor_blocks.shape[-1]
    rows = parts * piece_rows
    columns = total_columns // parts
    chips = span // (piece_rows * 2)
    factor = factor_blocks.reshape(entries, rows, span)
    inverse = diag_inverses.reshape(blocks, rows, span)
    block_rows, block_cols = block_index[:, 0], block_index[:, 1]
    numbers = jnp.arange(blocks, dtype=jnp.int32)
    row_begin = jnp.sum((block_rows[None, :] < numbers[:, None]).astype(jnp.int32), axis=1)
    match = (block_rows[None, None, :] == numbers[:, None, None]) & (
        block_cols[None, None, :] == numbers[None, :, None]
    )
    places = jnp.arange(1, entries + 1, dtype=jnp.int32)
    table = jnp.sum(jnp.where(match, places, 0), axis=2) - 1

    split = rhs.reshape(blocks, piece_rows, parts, columns).transpose(2, 0, 1, 3)
    split = lax.all_to_all(split, ROWS, 0, 0, tiled=True)

    def rhs_of(current):
        return split[:, current].reshape(rows, columns)

    def gather_row(current, after):
        first = jnp.minimum(row_begin[current], entries - current)
        slots = table[current, :current]
        slots = jnp.where(slots >= 0, slots - first, -1)
        slab = lax.dynamic_slice(factor, (first, 0, 0), (current, rows, span))
        if after is not None:
            slab, after = lax.optimization_barrier((slab, after))
        return slots, lax.all_gather(slab, ROWS, axis=0)

    def gather_inverse(current, after):
        slab = inverse[current]
        if after is not None:
            slab, after = lax.optimization_barrier((slab, after))
        return lax.all_gather(slab, ROWS, axis=0)

    ahead = 3
    inverses = {0: gather_inverse(0, None)}
    factors = {}
    for current in range(1, ahead):
        factors[current] = gather_row(current, None)
        inverses[current] = gather_inverse(current, None)
    copies = jnp.broadcast_to(rhs_of(0)[None], (chips, rows, columns))
    history, pieces = [], []
    for current in range(blocks):
        gathered = spread(copies)
        coming = current + ahead
        if coming < blocks:
            factors[coming] = gather_row(coming, gathered)
            inverses[coming] = gather_inverse(coming, gathered)
        copies, piece = solve(gathered, inverses[current])
        pieces.append(piece)
        if current + 1 == blocks:
            break
        slots, row_factor = factors[current + 1]
        if history:
            earlier = update(slots[:-1], row_factor, history)
        else:
            earlier = jnp.zeros((rows, columns), jnp.float32)
        gathered = spread(copies)
        copies, whole = residual(slots, gathered, row_factor, rhs_of(current + 1), earlier)
        history.append(whole)

    out = jnp.stack(pieces).reshape(blocks, parts, piece_rows, columns).transpose(1, 0, 2, 3)
    out = lax.all_to_all(out, ROWS, 0, 0, tiled=True)
    return out.transpose(1, 2, 0, 3).reshape(blocks, piece_rows, total_columns)


def solution(mesh):
    cores = 2
    across, along = mesh.shape["prow"], mesh.shape["pcol"]
    grid = Mesh(mesh.devices.reshape(across, along // cores, cores), (ROWS, CHIPS, CORES))
    column = (CHIPS, CORES)
    in_specs = (
        P(None, (ROWS, CHIPS, CORES), None),
        P(None, None, column, None, ROWS),
        P(None, None, column, None, ROWS),
        P(),
    )
    out_specs = P(None, (ROWS, CHIPS, CORES), None)
    return jax.shard_map(shards, mesh=grid, in_specs=in_specs, out_specs=out_specs, check_vma=False)
```

```python
import jax
import jax.numpy as jnp
from jax import lax
from jax.experimental import pallas as pl
from jax.experimental.pallas import tpu as pltpu
from jax.sharding import Mesh, PartitionSpec as P

ROWS, CHIPS, CORES = "prow", "chip", "core"
LANES = 128
CHUNK_ROWS = ((0, 1), (2, 3), (4, 5), (6, 7), (8, 9), (10, 11))
CHUNK_AFTER = (None, None, 0, 2, 4, 6)


def spread(copies):
    received = lax.all_to_all(copies, CHIPS, 0, 0, tiled=True)
    return lax.all_gather(received, CORES, axis=0)


def lane_of(shape):
    return lax.broadcasted_iota(jnp.int32, shape, 1)


def pack(value, parts):
    height = value.shape[0] // parts
    spare = LANES // parts
    last = value[(parts - 1) * height :]
    lane = lane_of(last.shape)
    packed = []
    for part in range(parts - 1):
        moved = pltpu.roll(last, LANES - spare - spare * part, 1)
        packed.append(
            jnp.where(lane < LANES - spare, value[part * height : (part + 1) * height], moved)
        )
    return jnp.concatenate(packed, axis=0).astype(jnp.bfloat16)


def copy_out(value, copies):
    for chip in range(copies.shape[0]):
        copies[chip] = value


def interleave(gathered, whole):
    cores, chips, height, _ = gathered.shape

    def place(chip, carry):
        for core in range(cores):
            first = pl.multiple_of((chip * cores + core) * 16, 16)
            for part in range(height // 16):
                whole[part, pl.ds(first, 16), :] = gathered[core, chip, pl.ds(part * 16, 16), :]
        return carry

    lax.fori_loop(0, chips, place, 0, unroll=8)


def raw_products(matrix, whole):
    parts = matrix.shape[0]
    last = matrix[parts - 1]
    return [
        jnp.dot(
            jnp.concatenate([matrix[part], last], axis=0),
            whole[part],
            preferred_element_type=jnp.float32,
        )
        for part in range(parts - 1)
    ]


def combine(raw):
    rows = raw[0].shape[0] // 2
    parts = len(raw) + 1
    spare = LANES // parts
    total = raw[0][:rows]
    for term in raw[1:]:
        total = total + term[:rows]
    lane = lane_of(total.shape)
    extra = pltpu.roll(raw[-1][rows:], spare * len(raw), 1)
    for part in reversed(range(len(raw) - 1)):
        moved = pltpu.roll(raw[part][rows:], spare * (part + 1), 1)
        extra = jnp.where(lane < spare * (part + 1), moved, extra)
    return total + extra


def widen(value, wide):
    wide[...] = jnp.zeros_like(wide)
    wide[:, pl.ds(0, value.shape[1])] = value
    return wide[...]


def start_entry(entry, chunks, spans, target, sem):
    for chunk, (low, high, offset) in zip(chunks, spans):

        @pl.when((entry >= low) & (entry < high))
        def _(chunk=chunk, low=low, high=high, offset=offset):
            place = jnp.clip(entry - low, 0, high - low - 1) + offset
            pltpu.make_async_copy(chunk.at[:, place], target, sem).start()


def wait_entry(chunks, target, sem):
    pltpu.make_async_copy(chunks[0].at[:, 0], target, sem).wait()


def first_kernel(rhs, copies, wide):
    parts, _, height, columns = rhs.shape
    value = rhs[:, 0].astype(jnp.float32).reshape(parts * height, columns)
    copy_out(pack(widen(value, wide), parts), copies)


def solve_kernel(current, place, gathered, chunk, *refs):
    if current:
        refs = refs[1:]
    copies, pieces, whole, matrix, sem = refs
    parts, _, height, columns = pieces.shape
    load = pltpu.make_async_copy(chunk.at[:, place], matrix, sem)
    load.start()
    interleave(gathered, whole)
    load.wait()
    value = combine(raw_products(matrix, whole))
    pieces[:, current] = value[:, :columns].astype(jnp.bfloat16).reshape(parts, height, columns)
    copy_out(pack(value, parts), copies)


def residual_kernel(current, spans, slots, gathered, rhs, *refs):
    count = len(spans)
    chunks, refs = refs[:count], refs[count:]
    parts, blocks, height, columns = rhs.shape
    keeps = current + 1 < blocks
    if current > 1:
        earlier, refs = refs[0], refs[1 + keeps :]
    copies, refs = refs[0], refs[1:]
    if keeps:
        history, refs = refs[0], refs[1:]
    whole, matrix, wide, total, sems = refs
    entry = slots[current - 1]
    start_entry(entry, chunks, spans, matrix, sems.at[0])
    interleave(gathered, whole)
    if keeps:
        keep = pltpu.make_async_copy(whole, history.at[current - 1], sems.at[1])
        keep.start()
    value = rhs[:, current].astype(jnp.float32).reshape(parts * height, columns)
    value = widen(value, wide)
    if current > 1:
        total[...] = earlier[...]
    else:
        total[...] = jnp.zeros_like(total)

    @pl.when(entry >= 0)
    def _():
        wait_entry(chunks, matrix, sems.at[0])
        total[...] += combine(raw_products(matrix, whole))

    copy_out(pack(value - total[...], parts), copies)
    if keeps:
        keep.wait()


def update_kernel(spans, slots, history, *refs):
    chunks, refs = refs[: len(spans)], refs[len(spans) :]
    result, wholes, matrices, total, history_sems, factor_sems = refs
    count = wholes.shape[0]
    for column in range(count):
        entry = slots[column]

        @pl.when(entry >= 0)
        def _(column=column):
            pltpu.make_async_copy(
                history.at[column], wholes.at[column], history_sems.at[column]
            ).start()

        start_entry(entry, chunks, spans, matrices.at[column], factor_sems.at[column])

    total[...] = jnp.zeros_like(total)

    def add(column, carry):
        @pl.when(slots[column] >= 0)
        def _():
            wait_entry(chunks, matrices.at[column], factor_sems.at[column])
            pltpu.make_async_copy(
                history.at[0], wholes.at[column], history_sems.at[column]
            ).wait()
            for part, term in enumerate(raw_products(matrices.at[column], wholes.at[column])):
                total[part] += term

        return carry

    lax.fori_loop(0, count, add, 0)
    result[...] = combine([total[part] for part in range(total.shape[0])])


def vmem():
    return pl.BlockSpec(memory_space=pltpu.VMEM)


def smem():
    return pl.BlockSpec(memory_space=pltpu.SMEM)


def anywhere():
    return pl.BlockSpec(memory_space=pl.ANY)


def in_vmem(array):
    return pltpu.with_memory_space_constraint(array, pltpu.VMEM)


def in_hbm(array):
    return pltpu.with_memory_space_constraint(array, pltpu.HBM)


LIMIT = pltpu.CompilerParams(vmem_limit_bytes=24 * 1024 * 1024)


def shards(rhs, factor_blocks, diag_inverses, block_index):
    blocks, height, total_columns = rhs.shape
    entries, parts = factor_blocks.shape[:2]
    span = factor_blocks.shape[-1]
    rows = parts * height
    columns = total_columns // parts
    cores = 2
    chips = span // (height * cores)
    packed = (parts - 1) * height
    factor = factor_blocks.reshape(entries, rows, span)
    inverse = diag_inverses.reshape(blocks, rows, span)
    block_rows, block_cols = block_index[:, 0], block_index[:, 1]
    numbers = jnp.arange(blocks, dtype=jnp.int32)
    match = (block_rows[None, None, :] == numbers[:, None, None]) & (
        block_cols[None, None, :] == numbers[None, :, None]
    )
    places = jnp.arange(1, entries + 1, dtype=jnp.int32)
    table = jnp.sum(jnp.where(match, places, 0), axis=2) - 1

    wholes = jax.ShapeDtypeStruct((parts - 1, span, LANES), jnp.bfloat16)
    copies_shape = pltpu.VMEM((chips, packed, LANES), jnp.bfloat16)
    pieces_shape = pltpu.VMEM((parts, blocks, height, columns), jnp.bfloat16)
    history_shape = pltpu.HBM((blocks - 2,) + wholes.shape, jnp.bfloat16)
    whole_scratch = pltpu.VMEM(wholes.shape, jnp.bfloat16)
    matrix_scratch = pltpu.VMEM((parts, rows, span), jnp.bfloat16)
    wide_scratch = pltpu.VMEM((rows, LANES), jnp.float32)

    def most(last):
        return min(entries, last * (last + 1) // 2)

    bounds = [0] + [most(last) for _, last in CHUNK_ROWS]
    bounds[-2] = (bounds[-3] + entries) // 2
    sizes = [last + 1 - first for first, last in CHUNK_ROWS]
    spans = [(low, high, size) for low, high, size in zip(bounds, bounds[1:], sizes)]
    chunks = [None] * len(spans)

    def gather_chunk(number, after):
        first, last = CHUNK_ROWS[number]
        low, high, _ = spans[number]
        slab = jnp.concatenate([inverse[first : last + 1], factor[low:high]], axis=0)
        if after is not None:
            slab, after = lax.optimization_barrier((slab, after))
        chunks[number] = lax.all_gather(slab, ROWS, axis=0)

    def chunks_of(current):
        high = most(current)
        low = max(0, entries - sum(range(current, blocks)))
        return [k for k, (a, b, _) in enumerate(spans) if a < high and b > low]

    def first(split):
        return pl.pallas_call(
            first_kernel,
            out_shape=copies_shape,
            in_specs=[vmem()],
            out_specs=vmem(),
            scratch_shapes=[wide_scratch],
            compiler_params=LIMIT,
            name="first",
        )(in_vmem(split))

    def solve(current, gathered, pieces):
        number = next(k for k, (a, b) in enumerate(CHUNK_ROWS) if a <= current <= b)
        place = current - CHUNK_ROWS[number][0]
        operands = [in_vmem(gathered), in_hbm(chunks[number])] + ([in_vmem(pieces)] if current else [])
        return pl.pallas_call(
            lambda *refs: solve_kernel(current, place, *refs),
            out_shape=(copies_shape, pieces_shape),
            in_specs=[vmem(), anywhere()] + ([vmem()] if current else []),
            out_specs=(vmem(), vmem()),
            input_output_aliases={2: 1} if current else {},
            scratch_shapes=[
                whole_scratch,
                matrix_scratch,
                pltpu.SemaphoreType.DMA,
            ],
            compiler_params=LIMIT,
            name="solve",
        )(*operands)

    def residual(current, gathered, split, earlier, history):
        used = chunks_of(current)
        keeps = current + 1 < blocks
        tail = [in_vmem(earlier)] if current > 1 else []
        if keeps and current > 1:
            tail.append(in_hbm(history))
        return pl.pallas_call(
            lambda *refs: residual_kernel(current, [spans[k] for k in used], *refs),
            out_shape=(copies_shape, history_shape) if keeps else (copies_shape,),
            in_specs=[smem(), vmem(), vmem()]
            + [anywhere()] * len(used)
            + [vmem(), anywhere()][: len(tail)],
            out_specs=(vmem(), anywhere()) if keeps else (vmem(),),
            input_output_aliases={4 + len(used): 1} if len(tail) > 1 else {},
            scratch_shapes=[
                whole_scratch,
                matrix_scratch,
                wide_scratch,
                wide_scratch,
                pltpu.SemaphoreType.DMA((2,)),
            ],
            compiler_params=LIMIT,
            name="residual",
        )(
            table[current],
            in_vmem(gathered),
            in_vmem(split),
            *[in_hbm(chunks[k]) for k in used],
            *tail,
        )

    def update(current, history):
        used = chunks_of(current)
        count = current - 1
        return pl.pallas_call(
            lambda *refs: update_kernel([spans[k] for k in used], *refs),
            out_shape=pltpu.VMEM((rows, LANES), jnp.float32),
            in_specs=[smem(), anywhere()] + [anywhere()] * len(used),
            out_specs=vmem(),
            scratch_shapes=[
                pltpu.VMEM((count,) + wholes.shape, jnp.bfloat16),
                pltpu.VMEM((count, parts, rows, span), jnp.bfloat16),
                pltpu.VMEM((parts - 1, 2 * rows, LANES), jnp.float32),
                pltpu.SemaphoreType.DMA((count,)),
                pltpu.SemaphoreType.DMA((count,)),
            ],
            compiler_params=LIMIT,
            cost_estimate=pl.CostEstimate(
                flops=count * 2 * rows * parts * span * 256,
                bytes_accessed=count * parts * span * (rows + LANES) * 2,
                transcendentals=0,
            ),
            name="update",
        )(table[current], in_hbm(history), *[in_hbm(chunks[k]) for k in used])

    split = rhs.reshape(blocks, height, parts, columns).transpose(2, 0, 1, 3)
    split = lax.all_to_all(split, ROWS, 0, 0, tiled=True)
    for number, after in enumerate(CHUNK_AFTER):
        if after is None:
            gather_chunk(number, None)
    copies = first(split)
    history = pieces = earlier = None
    for current in range(blocks):
        gathered = spread(copies)
        for number, after in enumerate(CHUNK_AFTER):
            if after == current:
                gather_chunk(number, gathered)
        copies, pieces = solve(current, gathered, pieces)
        if current + 1 == blocks:
            break
        if current:
            earlier = update(current + 1, history)
        gathered = spread(copies)
        copies, *history_after = residual(current + 1, gathered, split, earlier, history)
        history = history_after[0] if history_after else None

    out = lax.all_to_all(pieces, ROWS, 0, 0, tiled=True)
    return out.transpose(1, 2, 0, 3).reshape(blocks, height, total_columns)


def solution(mesh):
    cores = 2
    across, along = mesh.shape["prow"], mesh.shape["pcol"]
    grid = Mesh(mesh.devices.reshape(across, along // cores, cores), (ROWS, CHIPS, CORES))
    column = (CHIPS, CORES)
    in_specs = (
        P(None, (ROWS, CHIPS, CORES), None),
        P(None, None, column, None, ROWS),
        P(None, None, column, None, ROWS),
        P(),
    )
    out_specs = P(None, (ROWS, CHIPS, CORES), None)
    return jax.shard_map(shards, mesh=grid, in_specs=in_specs, out_specs=out_specs, check_vma=False)
```

```python
import jax
import jax.numpy as jnp
from jax import lax
from jax.experimental import pallas as pl
from jax.experimental.pallas import tpu as pltpu
from jax.sharding import Mesh, PartitionSpec as P

ROWS, CHIPS, CORES = "prow", "chip", "core"
LANES = 128
CHUNK_ROWS = ((0, 1), (2, 3), (4, 5), (6, 7), (8, 9), (10, 11))
CHUNK_AFTER = (None, None, 0, 2, 4, 7)


def exchange(copies):
    return lax.all_to_all(copies, CHIPS, 0, 0, tiled=True)


def other_core(array):
    return lax.ppermute(array, CORES, [(0, 1), (1, 0)])


def lane_of(shape):
    return lax.broadcasted_iota(jnp.int32, shape, 1)


def pack(value):
    lane = lane_of((16, LANES))

    def tile(core, part):
        first = (core * 4 + part) * 16
        return value[first : first + 16]

    def head(core):
        return jnp.where(
            lane < 48,
            tile(core, 0),
            jnp.where(lane < 96, pltpu.roll(tile(core, 1), 48, 1), pltpu.roll(tile(core, 2), 96, 1)),
        )

    low = jnp.where(lane < 16, pltpu.roll(tile(0, 2), 96, 1), pltpu.roll(tile(0, 3), 16, 1))
    high = jnp.where(lane < 80, pltpu.roll(tile(1, 2), 32, 1), pltpu.roll(tile(1, 3), 80, 1))
    tail = jnp.where(lane < 64, low, high)
    return jnp.concatenate([head(0), head(1), tail], axis=0).astype(jnp.bfloat16)


def unpack(gathered, whole):
    def place(chip, carry):
        first = pl.multiple_of(chip * 32, 32)
        whole[pl.ds(first, 32), pl.ds(0, LANES)] = gathered[chip, pl.ds(0, 32), :]
        tail = gathered[chip, pl.ds(32, 16), :]
        moved = pltpu.roll(tail.astype(jnp.float32), 64, 1).astype(jnp.bfloat16)
        whole[pl.ds(first, 16), pl.ds(LANES, LANES)] = tail
        whole[pl.ds(first + 16, 16), pl.ds(LANES, LANES)] = moved
        return carry

    lax.fori_loop(0, gathered.shape[0], place, 0, unroll=8)


def unpack_both(own, other, whole):
    low = lane_of((16, LANES)) < 64

    def place(chip, carry):
        first = pl.multiple_of(chip * 32, 32)
        whole[pl.ds(first, 32), pl.ds(0, LANES)] = own[chip, pl.ds(0, 32), :]
        whole[pl.ds(first, 32), pl.ds(LANES, LANES)] = other[chip, pl.ds(0, 32), :]
        one = own[chip, pl.ds(32, 16), :].astype(jnp.float32)
        two = other[chip, pl.ds(32, 16), :].astype(jnp.float32)
        tails = jnp.where(low, one, pltpu.roll(two, 64, 1))
        whole[pl.ds(first, 16), pl.ds(2 * LANES, LANES)] = tails.astype(jnp.bfloat16)
        tails = jnp.where(low, pltpu.roll(one, 64, 1), two)
        whole[pl.ds(first + 16, 16), pl.ds(2 * LANES, LANES)] = tails.astype(jnp.bfloat16)
        return carry

    lax.fori_loop(0, own.shape[0], place, 0, unroll=8)


def combine(raw, rows, head=0, tail=LANES, shift=0):
    def of(part, lanes):
        return raw[part * rows : (part + 1) * rows, lanes : lanes + LANES]

    def moved(value, by):
        return pltpu.roll(value, by % LANES, 1)

    second = jnp.where(
        lane_of((rows, LANES)) < 32, moved(of(2, head), 32), moved(of(2, tail), 32 - shift)
    )
    first = of(0, head) + moved(of(1, head), 80)
    return first + (second + moved(of(3, tail), 112 - shift))


def chain_product(own, other, which, whole):
    _, parts, rows, _ = own.shape
    stacked = jnp.concatenate(
        [matrices[which, part] for part in range(parts) for matrices in (own, other)], axis=0
    )
    raw = jnp.dot(stacked, whole[...], preferred_element_type=jnp.float32)
    return combine(raw, 2 * rows)


def core_rows(rows):
    core = lax.axis_index(CORES)
    return (
        pl.ds(pl.multiple_of(core * rows, rows), rows),
        pl.ds(pl.multiple_of((1 - core) * rows, rows), rows),
    )


def copy_out(value, packed, copies, sem):
    packed[...] = value
    for chip in range(copies.shape[0]):
        pltpu.make_async_copy(packed, copies.at[chip], sem).start()
    pltpu.make_async_copy(copies, copies, sem).wait()


def widen(rhs, wide):
    members, height, columns = rhs.shape
    wide[...] = jnp.zeros_like(wide)
    for member in range(members):
        part, core = member // 2, member % 2
        wide[pl.ds((core * 4 + part) * height, height), pl.ds(0, columns)] = rhs[
            member
        ].astype(jnp.float32)


def start_entry(entry, chunks, spans, target, sem):
    for chunk, (low, high, offset) in zip(chunks, spans):

        @pl.when((entry >= low) & (entry < high))
        def _(chunk=chunk, low=low, high=high, offset=offset):
            place = jnp.clip(entry - low, 0, high - low - 1) + offset
            pltpu.make_async_copy(chunk.at[:, place], target, sem).start()


def wait_entry(chunks, target, sem):
    pltpu.make_async_copy(chunks[0].at[:, 0], target, sem).wait()


def first_kernel(rhs, copies, wide, packed, sem, own, own_sem):
    load = pltpu.make_async_copy(rhs.at[:, 0], own, own_sem)
    load.start()
    load.wait()
    widen(own, wide)
    copy_out(pack(wide[...]), packed, copies, sem)


def pick_kernel(current, place, spans, slots, own, *refs):
    chunks, (blocks, sems) = refs[: len(spans)], refs[len(spans) :]
    load = pltpu.make_async_copy(own.at[:, place], blocks.at[0], sems.at[0])
    load.start()
    if current:
        entry = slots[current - 1]
        start_entry(entry, chunks, spans, blocks.at[1], sems.at[1])

        @pl.when(entry < 0)
        def _():
            blocks[1] = jnp.zeros_like(blocks[1])

        @pl.when(entry >= 0)
        def _():
            wait_entry(chunks, blocks.at[1], sems.at[1])

    load.wait()


def hold_kernel(there, here, sem):
    load = pltpu.make_async_copy(there, here, sem)
    load.start()
    load.wait()


def solve_kernel(current, gathered, own, other, *refs):
    if current:
        refs = refs[1:]
    copies, pieces, whole, total, packed, sem, piece, piece_sem = refs
    members, blocks, height, columns = pieces.shape
    rows = own.shape[2]
    unpack(gathered, whole)
    value = chain_product(own, other, 0, whole)
    for number, place in enumerate(core_rows(rows)):
        total[place, :] = value[number * rows : (number + 1) * rows]
    value = total[...]
    rounded = value[:, :columns].astype(jnp.bfloat16)
    for member in range(members):
        first = (member % 2 * 4 + member // 2) * height
        piece[member] = rounded[first : first + height]
    keep = pltpu.make_async_copy(piece, pieces.at[:, current], piece_sem)
    keep.start()
    if current + 1 < blocks:
        copy_out(pack(value), packed, copies, sem)
    keep.wait()


def residual_kernel(current, gathered, own, other, rhs, *refs):
    if current > 1:
        sums, others, refs = refs[0], refs[1], refs[2:]
    copies, refs = refs[0], refs[1:]
    keeps = current + 1 < rhs.shape[1]
    if keeps:
        kept, refs = refs[0], refs[1:]
    whole, total, packed, sem, piece, piece_sem, earlier, sems, keep_sem = refs
    loads = [pltpu.make_async_copy(rhs.at[:, current], piece, piece_sem)]
    if current > 1:
        for core, array in enumerate((sums.at[0], others)):
            loads.append(pltpu.make_async_copy(array, earlier.at[core], sems.at[core]))
    for load in loads:
        load.start()
    if keeps:
        keep = pltpu.make_async_copy(gathered, kept, keep_sem)
        keep.start()
    rows = own.shape[2]
    places = core_rows(rows)
    unpack(gathered, whole)
    value = chain_product(own, other, 1, whole)
    for load in loads:
        load.wait()
    widen(piece, total)
    if current > 1:
        for core, place in enumerate(places):
            total[place, :] -= earlier[core]
    for number, place in enumerate(places):
        total[place, :] -= value[number * rows : (number + 1) * rows]

    copy_out(pack(total[...]), packed, copies, sem)
    if keeps:
        keep.wait()


def update_kernel(spans, keeps, slots, own, other, *refs):
    result, refs_in, refs = refs[-9 - keeps], refs[: -9 - keeps], refs[-8 - keeps :]
    history, chunks = refs_in[: -len(spans)], refs_in[-len(spans) :]
    if keeps:
        kept, refs = refs[0], refs[1:]
    wholes, matrices, total, received, summed, sems, factor_sems, received_sems = refs
    count, parts, rows, span = matrices.shape
    newest = count - 1
    arrivals = [
        pltpu.make_async_copy(array, received.at[core], received_sems.at[core])
        for core, array in enumerate((own, other))
    ]
    for arrival in arrivals:
        arrival.start()
    for column in range(count):
        entry = slots[column]
        start_entry(entry, chunks, spans, matrices.at[column], factor_sems.at[column])
        if column < newest:

            @pl.when(entry >= 0)
            def _(column=column):
                pltpu.make_async_copy(
                    history[column], wholes.at[column], sems.at[column]
                ).start()

    for arrival in arrivals:
        arrival.wait()
    unpack_both(received.at[0], received.at[1], wholes.at[newest])
    if keeps:
        keep = pltpu.make_async_copy(wholes.at[newest], kept, sems.at[newest])
        keep.start()
    total[...] = jnp.zeros_like(total)

    def add(column):
        wait_entry(chunks, matrices.at[column], factor_sems.at[column])
        total[...] += jnp.dot(
            matrices[column].reshape(parts * rows, span),
            wholes[column],
            preferred_element_type=jnp.float32,
        )

    def add_earlier(column, carry):
        @pl.when(slots[column] >= 0)
        def _():
            pltpu.make_async_copy(history[0], wholes.at[column], sems.at[column]).wait()
            add(column)

        return carry

    if newest:
        lax.fori_loop(0, newest, add_earlier, 0)

    @pl.when(slots[newest] >= 0)
    def _():
        add(newest)

    raw = total[...]
    for core in range(2):
        summed[core] = combine(raw, rows, core * LANES, 2 * LANES, core * 64)
    store = pltpu.make_async_copy(summed, result, received_sems.at[0])
    store.start()
    store.wait()
    if keeps:
        keep.wait()


def vmem():
    return pl.BlockSpec(memory_space=pltpu.VMEM)


def smem():
    return pl.BlockSpec(memory_space=pltpu.SMEM)


def anywhere():
    return pl.BlockSpec(memory_space=pl.ANY)


def in_vmem(array):
    return pltpu.with_memory_space_constraint(array, pltpu.VMEM)


def in_hbm(array):
    return pltpu.with_memory_space_constraint(array, pltpu.HBM)


LIMIT = pltpu.CompilerParams(vmem_limit_bytes=24 * 1024 * 1024)


def shards(rhs, factor_blocks, diag_inverses, block_index):
    blocks, height, total_columns = rhs.shape
    entries, parts = factor_blocks.shape[:2]
    span = factor_blocks.shape[-1]
    cores = 2
    members = parts * cores
    rows = parts * height
    columns = total_columns // members
    chips = span // (height * cores)
    factor = factor_blocks.reshape(entries, rows, span)
    inverse = diag_inverses.reshape(blocks, rows, span)
    block_rows, block_cols = block_index[:, 0], block_index[:, 1]
    numbers = jnp.arange(blocks, dtype=jnp.int32)
    match = (block_rows[None, None, :] == numbers[:, None, None]) & (
        block_cols[None, None, :] == numbers[None, :, None]
    )
    places = jnp.arange(1, entries + 1, dtype=jnp.int32)
    table = jnp.sum(jnp.where(match, places, 0), axis=2) - 1

    copies_shape = pltpu.HBM((chips, 48, LANES), jnp.bfloat16)
    copy_scratch = [pltpu.VMEM((48, LANES), jnp.bfloat16), pltpu.SemaphoreType.DMA]
    piece_scratch = [
        pltpu.VMEM((members, height, columns), jnp.bfloat16),
        pltpu.SemaphoreType.DMA,
    ]
    pieces_shape = pltpu.HBM((members, blocks, height, columns), jnp.bfloat16)
    history_shape = pltpu.HBM((span, 3 * LANES), jnp.bfloat16)
    sums_shape = pltpu.HBM((cores, rows, LANES), jnp.float32)
    whole_scratch = pltpu.VMEM((span, 2 * LANES), jnp.bfloat16)
    wide_scratch = pltpu.VMEM((cores * rows, LANES), jnp.float32)

    def most(last):
        return min(entries, last * (last + 1) // 2)

    bounds = [0] + [most(last) for _, last in CHUNK_ROWS]
    sizes = [last + 1 - first for first, last in CHUNK_ROWS]
    spans = [(low, high, size) for low, high, size in zip(bounds, bounds[1:], sizes)]
    chunks = [None] * len(spans)

    def gather_chunk(number, after):
        first, last = CHUNK_ROWS[number]
        low, high, _ = spans[number]
        slab = jnp.concatenate([inverse[first : last + 1], factor[low:high]], axis=0)
        if after is not None:
            slab, after = lax.optimization_barrier((slab, after))
        chunks[number] = lax.all_gather(slab, ROWS, axis=0)

    def chunks_of(current):
        high = most(current)
        low = max(0, entries - sum(range(current, blocks)))
        return [k for k, (a, b, _) in enumerate(spans) if a < high and b > low]

    def first(split):
        return pl.pallas_call(
            first_kernel,
            out_shape=copies_shape,
            in_specs=[anywhere()],
            out_specs=anywhere(),
            scratch_shapes=[wide_scratch, *copy_scratch, *piece_scratch],
            compiler_params=LIMIT,
            name="first",
        )(in_hbm(split))

    def pick(current):
        number = next(k for k, (a, b) in enumerate(CHUNK_ROWS) if a <= current <= b)
        place = current - CHUNK_ROWS[number][0]
        used = chunks_of(current) if current else []
        kinds = 2 if current else 1
        picked = pl.pallas_call(
            lambda *refs: pick_kernel(current, place, [spans[k] for k in used], *refs),
            out_shape=pltpu.VMEM((kinds, parts, rows, span), jnp.bfloat16),
            in_specs=[smem(), anywhere()] + [anywhere()] * len(used),
            out_specs=vmem(),
            scratch_shapes=[pltpu.SemaphoreType.DMA((2,))],
            compiler_params=LIMIT,
            cost_estimate=pl.CostEstimate(
                flops=0, bytes_accessed=2 * kinds * parts * rows * span * 2, transcendentals=0
            ),
            name="pick",
        )(table[current], in_hbm(chunks[number]), *[in_hbm(chunks[k]) for k in used])
        return picked, hold(other_core(picked))

    def hold(array):
        return pl.pallas_call(
            hold_kernel,
            out_shape=pltpu.VMEM(array.shape, array.dtype),
            in_specs=[anywhere()],
            out_specs=vmem(),
            scratch_shapes=[pltpu.SemaphoreType.DMA],
            compiler_params=LIMIT,
            cost_estimate=pl.CostEstimate(
                flops=0, bytes_accessed=4 * array.size, transcendentals=0
            ),
            name="hold",
        )(array)

    def solve(current, gathered, picked, pieces):
        operands = [in_vmem(array) for array in (gathered, *picked)]
        if current:
            operands.append(in_hbm(pieces))
        return pl.pallas_call(
            lambda *refs: solve_kernel(current, *refs),
            out_shape=(copies_shape, pieces_shape),
            in_specs=[vmem(), vmem(), vmem(), anywhere()][: len(operands)],
            out_specs=(anywhere(), anywhere()),
            input_output_aliases={3: 1} if current else {},
            scratch_shapes=[whole_scratch, wide_scratch, *copy_scratch, *piece_scratch],
            compiler_params=LIMIT,
            name="solve",
        )(*operands)

    def residual(current, gathered, picked, split, earlier):
        held = [in_vmem(array) for array in (gathered, *picked)]
        operands = [in_hbm(split)]
        if current > 1:
            operands += [in_hbm(array) for array in earlier]
        outputs = 2 if current + 1 < blocks else 1
        return pl.pallas_call(
            lambda *refs: residual_kernel(current, *refs),
            out_shape=(copies_shape,) * outputs,
            in_specs=[vmem()] * 3 + [anywhere()] * len(operands),
            out_specs=(anywhere(),) * outputs,
            scratch_shapes=[
                whole_scratch,
                wide_scratch,
                *copy_scratch,
                *piece_scratch,
                pltpu.VMEM((cores, rows, LANES), jnp.float32),
                pltpu.SemaphoreType.DMA((2,)),
                pltpu.SemaphoreType.DMA,
            ],
            compiler_params=LIMIT,
            name="residual",
        )(*held, *operands)

    def update(current, newest, history):
        used = chunks_of(current)
        count = current - 1
        keeps = current + 1 < blocks
        before = [in_hbm(array) for array in history]
        result = pl.pallas_call(
            lambda *refs: update_kernel([spans[k] for k in used], keeps, *refs),
            out_shape=(sums_shape, history_shape) if keeps else (sums_shape,),
            in_specs=[smem()] + [anywhere()] * (2 + len(before) + len(used)),
            out_specs=(anywhere(),) * (1 + keeps),
            scratch_shapes=[
                pltpu.VMEM((count, span, 3 * LANES), jnp.bfloat16),
                pltpu.VMEM((count, parts, rows, span), jnp.bfloat16),
                pltpu.VMEM((parts * rows, 3 * LANES), jnp.float32),
                pltpu.VMEM((cores, chips, 48, LANES), jnp.bfloat16),
                pltpu.VMEM((cores, rows, LANES), jnp.float32),
                pltpu.SemaphoreType.DMA((count,)),
                pltpu.SemaphoreType.DMA((count,)),
                pltpu.SemaphoreType.DMA((2,)),
            ],
            compiler_params=LIMIT,
            cost_estimate=pl.CostEstimate(
                flops=count * 2 * cores * parts * rows * span * 256,
                bytes_accessed=count * parts * span * (rows + LANES) * 2,
                transcendentals=0,
            ),
            name="update",
        )(
            table[current],
            *[in_hbm(part) for part in newest],
            *before,
            *[in_hbm(chunks[k]) for k in used],
        )
        return result[0], history + list(result[1:])

    split = rhs.reshape(blocks, height, members, columns).transpose(2, 0, 1, 3)
    split = lax.all_to_all(split, (ROWS, CORES), 0, 0, tiled=True)
    for number, after in enumerate(CHUNK_AFTER):
        if after is None:
            gather_chunk(number, None)
    copies = first(split)
    picked = pick(0)
    pieces = earlier = None
    history = []
    starts = {first_row: number for number, (first_row, _) in enumerate(CHUNK_ROWS)}
    for current in range(blocks):
        last = current + 1 == blocks
        gathered = exchange(copies)
        for number, after in enumerate(CHUNK_AFTER):
            if after == current:
                gather_chunk(number, gathered)
        copies, pieces = solve(current, gathered, picked, pieces)
        if last:
            break
        if current == 1:
            chunks[1], copies = lax.optimization_barrier((chunks[1], copies))
        picked = pick(current + 1)
        gathered = exchange(copies)
        copies, *kept = residual(current + 1, gathered, picked, split, earlier)
        number = starts.get(current + 2)
        if number is not None and number > 1:
            chunks[number], copies = lax.optimization_barrier((chunks[number], copies))
        if current + 2 < blocks:
            sums, history = update(current + 2, (kept[0], other_core(kept[0])), history)
            earlier = sums, other_core(sums[1])

    out = lax.all_to_all(pieces, (ROWS, CORES), 0, 0, tiled=True)
    return out.transpose(1, 2, 0, 3).reshape(blocks, height, total_columns)


def solution(mesh):
    cores = 2
    across, along = mesh.shape["prow"], mesh.shape["pcol"]
    grid = Mesh(mesh.devices.reshape(across, along // cores, cores), (ROWS, CHIPS, CORES))
    column = (CHIPS, CORES)
    in_specs = (
        P(None, (ROWS, CHIPS, CORES), None),
        P(None, None, column, None, ROWS),
        P(None, None, column, None, ROWS),
        P(),
    )
    out_specs = P(None, (ROWS, CHIPS, CORES), None)
    return jax.shard_map(shards, mesh=grid, in_specs=in_specs, out_specs=out_specs, check_vma=False)
```

```python
import jax
import jax.numpy as jnp
from jax import lax
from jax.experimental import pallas as pl
from jax.experimental.pallas import tpu as pltpu
from jax.sharding import Mesh, PartitionSpec as P

ROWS, CHIPS, CORES = "prow", "chip", "core"
LANES = 128
CHUNK_ROWS = ((0, 1), (2, 3), (4, 5), (6, 7), (8, 8), (9, 11))
CHUNK_AFTER = (None, None, 0, 2, 4, 5)


def exchange(copies):
    return lax.all_to_all(copies, CHIPS, 0, 0, tiled=True)


def other_core(array):
    return lax.ppermute(array, CORES, [(0, 1), (1, 0)])


def lane_of(shape):
    return lax.broadcasted_iota(jnp.int32, shape, 1)


def pack(value):
    lane = lane_of((16, LANES))

    def tile(core, part):
        first = (core * 4 + part) * 16
        return value[first : first + 16]

    def head(core):
        return jnp.where(
            lane < 48,
            tile(core, 0),
            jnp.where(lane < 96, pltpu.roll(tile(core, 1), 48, 1), pltpu.roll(tile(core, 2), 96, 1)),
        )

    low = jnp.where(lane < 16, pltpu.roll(tile(0, 2), 96, 1), pltpu.roll(tile(0, 3), 16, 1))
    high = jnp.where(lane < 80, pltpu.roll(tile(1, 2), 32, 1), pltpu.roll(tile(1, 3), 80, 1))
    tail = jnp.where(lane < 64, low, high)
    return jnp.concatenate([head(0), head(1), tail], axis=0).astype(jnp.bfloat16)


def unpack(gathered, whole, unroll=32):
    def place(chip, carry):
        first = pl.multiple_of(chip * 32, 32)
        whole[pl.ds(first, 32), pl.ds(0, LANES)] = gathered[chip, pl.ds(0, 32), :]
        tail = gathered[chip, pl.ds(32, 16), :]
        moved = pltpu.roll(tail.astype(jnp.float32), 64, 1).astype(jnp.bfloat16)
        whole[pl.ds(first, 16), pl.ds(LANES, LANES)] = tail
        whole[pl.ds(first + 16, 16), pl.ds(LANES, LANES)] = moved
        return carry

    lax.fori_loop(0, gathered.shape[0], place, 0, unroll=unroll)


def unpack_both(own, other, whole):
    low = lane_of((16, LANES)) < 64

    def place(chip, carry):
        first = pl.multiple_of(chip * 32, 32)
        whole[pl.ds(first, 32), pl.ds(0, LANES)] = own[chip, pl.ds(0, 32), :]
        whole[pl.ds(first, 32), pl.ds(LANES, LANES)] = other[chip, pl.ds(0, 32), :]
        one = own[chip, pl.ds(32, 16), :].astype(jnp.float32)
        two = other[chip, pl.ds(32, 16), :].astype(jnp.float32)
        tails = jnp.where(low, one, pltpu.roll(two, 64, 1))
        whole[pl.ds(first, 16), pl.ds(2 * LANES, LANES)] = tails.astype(jnp.bfloat16)
        tails = jnp.where(low, pltpu.roll(one, 64, 1), two)
        whole[pl.ds(first + 16, 16), pl.ds(2 * LANES, LANES)] = tails.astype(jnp.bfloat16)
        return carry

    lax.fori_loop(0, own.shape[0], place, 0, unroll=8)


def combine(raw, rows, head=0, tail=LANES, shift=0):
    def of(part, lanes):
        return raw[part * rows : (part + 1) * rows, lanes : lanes + LANES]

    def moved(value, by):
        return pltpu.roll(value, by % LANES, 1)

    second = jnp.where(
        lane_of((rows, LANES)) < 32, moved(of(2, head), 32), moved(of(2, tail), 32 - shift)
    )
    first = of(0, head) + moved(of(1, head), 80)
    return first + (second + moved(of(3, tail), 112 - shift))


def chain_product(own, other, which, whole):
    _, parts, rows, _ = own.shape
    stacked = jnp.concatenate(
        [matrices[which, part] for part in range(parts) for matrices in (own, other)], axis=0
    )
    raw = jnp.dot(stacked, whole[...], preferred_element_type=jnp.float32)
    return combine(raw, 2 * rows)


def core_rows(rows):
    core = lax.axis_index(CORES)
    return (
        pl.ds(pl.multiple_of(core * rows, rows), rows),
        pl.ds(pl.multiple_of((1 - core) * rows, rows), rows),
    )


def copy_out(value, packed, copies, sem):
    packed[...] = value
    for chip in range(copies.shape[0]):
        pltpu.make_async_copy(packed, copies.at[chip], sem).start()
    pltpu.make_async_copy(copies, copies, sem).wait()


def widen(rhs, wide):
    members, height, columns = rhs.shape
    wide[...] = jnp.zeros_like(wide)
    for member in range(members):
        part, core = member // 2, member % 2
        wide[pl.ds((core * 4 + part) * height, height), pl.ds(0, columns)] = rhs[
            member
        ].astype(jnp.float32)


def start_entry(entry, chunks, spans, target, sem):
    for chunk, (low, high, offset) in zip(chunks, spans):

        @pl.when((entry >= low) & (entry < high))
        def _(chunk=chunk, low=low, high=high, offset=offset):
            place = jnp.clip(entry - low, 0, high - low - 1) + offset
            pltpu.make_async_copy(chunk.at[:, place], target, sem).start()


def wait_entry(chunks, target, sem):
    pltpu.make_async_copy(chunks[0].at[:, 0], target, sem).wait()


def first_kernel(rhs, copies, wide, packed, sem):
    widen(rhs[:, 0], wide)
    copy_out(pack(wide[...]), packed, copies, sem)


def pick_kernel(current, place, spans, own, *refs):
    if current:
        slots, refs = refs[0], refs[1:]
    chunks, (blocks, sems) = refs[: len(spans)], refs[len(spans) :]
    load = pltpu.make_async_copy(own.at[:, place], blocks.at[0], sems.at[0])
    load.start()
    if current:
        entry = slots[current - 1]
        start_entry(entry, chunks, spans, blocks.at[1], sems.at[1])

        @pl.when(entry < 0)
        def _():
            blocks[1] = jnp.zeros_like(blocks[1])

        @pl.when(entry >= 0)
        def _():
            wait_entry(chunks, blocks.at[1], sems.at[1])

    load.wait()


def hold_kernel(there, here, sem):
    load = pltpu.make_async_copy(there, here, sem)
    load.start()
    load.wait()


def solve_kernel(current, gathered, own, other, *refs):
    if current:
        refs = refs[1:]
    copies, pieces, whole, total, packed, sem, piece, piece_sem = refs
    members, blocks, height, columns = pieces.shape
    rows = own.shape[2]
    unpack(gathered, whole)
    value = chain_product(own, other, 0, whole)
    for number, place in enumerate(core_rows(rows)):
        total[place, :] = value[number * rows : (number + 1) * rows]
    value = total[...]
    rounded = value[:, :columns].astype(jnp.bfloat16)
    for member in range(members):
        first = (member % 2 * 4 + member // 2) * height
        piece[member] = rounded[first : first + height]
    keep = pltpu.make_async_copy(piece, pieces.at[:, current], piece_sem)
    keep.start()
    if current + 1 < blocks:
        copy_out(pack(value), packed, copies, sem)
    keep.wait()


def residual_kernel(current, gathered, own, other, rhs, *refs):
    if current > 1:
        sums, others, refs = refs[0], refs[1], refs[2:]
    copies, refs = refs[0], refs[1:]
    keeps = current + 1 < rhs.shape[1]
    if keeps:
        kept, refs = refs[0], refs[1:]
    whole, total, packed, sem, piece, piece_sem, earlier, sems, keep_sem = refs
    loads = [pltpu.make_async_copy(rhs.at[:, current], piece, piece_sem)]
    if current > 1:
        for core, array in enumerate((sums.at[0], others)):
            loads.append(pltpu.make_async_copy(array, earlier.at[core], sems.at[core]))
    for load in loads:
        load.start()
    rows = own.shape[2]
    places = core_rows(rows)
    if keeps:
        keep = pltpu.make_async_copy(gathered, kept, keep_sem)
        keep.start()
    unpack(gathered, whole, 8 if keeps else 32)
    value = chain_product(own, other, 1, whole)
    for load in loads:
        load.wait()
    widen(piece, total)
    if current > 1:
        for core, place in enumerate(places):
            total[place, :] -= earlier[core]
    for number, place in enumerate(places):
        total[place, :] -= value[number * rows : (number + 1) * rows]

    copy_out(pack(total[...]), packed, copies, sem)
    if keeps:
        keep.wait()


def update_kernel(spans, keeps, slots, own, other, *refs):
    result, refs_in, refs = refs[-9 - keeps], refs[: -9 - keeps], refs[-8 - keeps :]
    history, chunks = refs_in[: -len(spans)], refs_in[-len(spans) :]
    if keeps:
        kept, refs = refs[0], refs[1:]
    wholes, matrices, total, received, summed, sems, factor_sems, received_sems = refs
    count, parts, rows, span = matrices.shape
    newest = count - 1
    arrivals = [
        pltpu.make_async_copy(array, received.at[core], received_sems.at[core])
        for core, array in enumerate((own, other))
    ]
    for arrival in arrivals:
        arrival.start()

    def start_factor(column, carry):
        start_entry(slots[column], chunks, spans, matrices.at[column], factor_sems.at[column])
        return carry

    lax.fori_loop(0, count, start_factor, 0)
    for column in range(newest):

        @pl.when(slots[column] >= 0)
        def _(column=column):
            pltpu.make_async_copy(history[column], wholes.at[column], sems.at[column]).start()

    for arrival in arrivals:
        arrival.wait()
    unpack_both(received.at[0], received.at[1], wholes.at[newest])
    if keeps:
        keep = pltpu.make_async_copy(wholes.at[newest], kept, sems.at[newest])
        keep.start()
    total[...] = jnp.zeros_like(total)

    def add(column):
        wait_entry(chunks, matrices.at[column], factor_sems.at[column])
        total[...] += jnp.dot(
            matrices[column].reshape(parts * rows, span),
            wholes[column],
            preferred_element_type=jnp.float32,
        )

    def add_earlier(column, carry):
        @pl.when(slots[column] >= 0)
        def _():
            pltpu.make_async_copy(history[0], wholes.at[column], sems.at[column]).wait()
            add(column)

        return carry

    if newest:
        lax.fori_loop(0, newest, add_earlier, 0)

    @pl.when(slots[newest] >= 0)
    def _():
        add(newest)

    raw = total[...]
    for core in range(2):
        summed[core] = combine(raw, rows, core * LANES, 2 * LANES, core * 64)
    store = pltpu.make_async_copy(summed, result, received_sems.at[0])
    store.start()
    store.wait()
    if keeps:
        keep.wait()


def vmem():
    return pl.BlockSpec(memory_space=pltpu.VMEM)


def smem():
    return pl.BlockSpec(memory_space=pltpu.SMEM)


def anywhere():
    return pl.BlockSpec(memory_space=pl.ANY)


def in_vmem(array):
    return pltpu.with_memory_space_constraint(array, pltpu.VMEM)


def in_hbm(array):
    return pltpu.with_memory_space_constraint(array, pltpu.HBM)


LIMIT = pltpu.CompilerParams(vmem_limit_bytes=24 * 1024 * 1024)


def shards(rhs, factor_blocks, diag_inverses, block_index):
    blocks, height, total_columns = rhs.shape
    entries, parts = factor_blocks.shape[:2]
    span = factor_blocks.shape[-1]
    cores = 2
    members = parts * cores
    rows = parts * height
    columns = total_columns // members
    chips = span // (height * cores)
    factor = factor_blocks.reshape(entries, rows, span)
    inverse = diag_inverses.reshape(blocks, rows, span)
    copies_shape = pltpu.HBM((chips, 48, LANES), jnp.bfloat16)
    copy_scratch = [pltpu.VMEM((48, LANES), jnp.bfloat16), pltpu.SemaphoreType.DMA]
    piece_scratch = [
        pltpu.VMEM((members, height, columns), jnp.bfloat16),
        pltpu.SemaphoreType.DMA,
    ]
    pieces_shape = pltpu.HBM((members, blocks, height, columns), jnp.bfloat16)
    history_shape = pltpu.HBM((span, 3 * LANES), jnp.bfloat16)
    sums_shape = pltpu.HBM((cores, rows, LANES), jnp.float32)
    whole_scratch = pltpu.VMEM((span, 2 * LANES), jnp.bfloat16)
    wide_scratch = pltpu.VMEM((cores * rows, LANES), jnp.float32)

    def most(last):
        return min(entries, last * (last + 1) // 2)

    bounds = [0] + [most(last) for _, last in CHUNK_ROWS]
    sizes = [last + 1 - first for first, last in CHUNK_ROWS]
    spans = [(low, high, size) for low, high, size in zip(bounds, bounds[1:], sizes)]
    chunks = [None] * len(spans)

    def gather_chunk(number, after):
        first, last = CHUNK_ROWS[number]
        low, high, _ = spans[number]
        slab = jnp.concatenate([inverse[first : last + 1], factor[low:high]], axis=0)
        if after is not None:
            slab, after = lax.optimization_barrier((slab, after))
        chunks[number] = lax.all_gather(slab, ROWS, axis=0)

    def chunks_of(current):
        high = most(current)
        low = max(0, entries - sum(range(current, blocks)))
        return [k for k, (a, b, _) in enumerate(spans) if a < high and b > low]

    def first(split):
        return pl.pallas_call(
            first_kernel,
            out_shape=copies_shape,
            in_specs=[vmem()],
            out_specs=anywhere(),
            scratch_shapes=[wide_scratch, *copy_scratch],
            compiler_params=LIMIT,
            name="first",
        )(in_vmem(split))

    def pick(current):
        number = next(k for k, (a, b) in enumerate(CHUNK_ROWS) if a <= current <= b)
        place = current - CHUNK_ROWS[number][0]
        used = chunks_of(current) if current else []
        kinds = 2 if current else 1
        used_rows = [current] if current else []
        picked = pl.pallas_call(
            lambda *refs: pick_kernel(current, place, [spans[k] for k in used], *refs),
            out_shape=pltpu.VMEM((kinds, parts, rows, span), jnp.bfloat16),
            in_specs=[anywhere(), smem()][:kinds] + [anywhere()] * len(used),
            out_specs=vmem(),
            scratch_shapes=[pltpu.SemaphoreType.DMA((2,))],
            compiler_params=LIMIT,
            cost_estimate=pl.CostEstimate(
                flops=0, bytes_accessed=2 * kinds * parts * rows * span * 2, transcendentals=0
            ),
            name="pick",
        )(
            in_hbm(chunks[number]), *[table[k] for k in used_rows], *[in_hbm(chunks[k]) for k in used]
        )
        return picked, hold(other_core(picked))

    def hold(array):
        return pl.pallas_call(
            hold_kernel,
            out_shape=pltpu.VMEM(array.shape, array.dtype),
            in_specs=[anywhere()],
            out_specs=vmem(),
            scratch_shapes=[pltpu.SemaphoreType.DMA],
            compiler_params=LIMIT,
            cost_estimate=pl.CostEstimate(
                flops=0, bytes_accessed=4 * array.size, transcendentals=0
            ),
            name="hold",
        )(array)

    def solve(current, gathered, picked, pieces):
        operands = [in_vmem(array) for array in (gathered, *picked)]
        if current:
            operands.append(in_hbm(pieces))
        return pl.pallas_call(
            lambda *refs: solve_kernel(current, *refs),
            out_shape=(copies_shape, pieces_shape),
            in_specs=[vmem(), vmem(), vmem(), anywhere()][: len(operands)],
            out_specs=(anywhere(), anywhere()),
            input_output_aliases={3: 1} if current else {},
            scratch_shapes=[whole_scratch, wide_scratch, *copy_scratch, *piece_scratch],
            compiler_params=LIMIT,
            name="solve",
        )(*operands)

    def residual(current, gathered, picked, split, earlier):
        held = [in_vmem(array) for array in (gathered, *picked)]
        operands = [in_hbm(split)]
        if current > 1:
            operands += [in_hbm(array) for array in earlier]
        outputs = 2 if current + 1 < blocks else 1
        return pl.pallas_call(
            lambda *refs: residual_kernel(current, *refs),
            out_shape=(copies_shape,) * outputs,
            in_specs=[vmem()] * 3 + [anywhere()] * len(operands),
            out_specs=(anywhere(),) * outputs,
            scratch_shapes=[
                whole_scratch,
                wide_scratch,
                *copy_scratch,
                *piece_scratch,
                pltpu.VMEM((cores, rows, LANES), jnp.float32),
                pltpu.SemaphoreType.DMA((2,)),
                pltpu.SemaphoreType.DMA,
            ],
            compiler_params=LIMIT,
            name="residual",
        )(*held, *operands)

    def update(current, newest, history):
        used = chunks_of(current)
        count = current - 1
        keeps = current + 1 < blocks
        before = [in_hbm(array) for array in history]
        result = pl.pallas_call(
            lambda *refs: update_kernel([spans[k] for k in used], keeps, *refs),
            out_shape=(sums_shape, history_shape) if keeps else (sums_shape,),
            in_specs=[smem()] + [anywhere()] * (2 + len(before) + len(used)),
            out_specs=(anywhere(),) * (1 + keeps),
            scratch_shapes=[
                pltpu.VMEM((count, span, 3 * LANES), jnp.bfloat16),
                pltpu.VMEM((count, parts, rows, span), jnp.bfloat16),
                pltpu.VMEM((parts * rows, 3 * LANES), jnp.float32),
                pltpu.VMEM((cores, chips, 48, LANES), jnp.bfloat16),
                pltpu.VMEM((cores, rows, LANES), jnp.float32),
                pltpu.SemaphoreType.DMA((count,)),
                pltpu.SemaphoreType.DMA((count,)),
                pltpu.SemaphoreType.DMA((2,)),
            ],
            compiler_params=LIMIT,
            cost_estimate=pl.CostEstimate(
                flops=count * 2 * cores * parts * rows * span * 256,
                bytes_accessed=count * parts * span * (rows + LANES) * 2,
                transcendentals=0,
            ),
            name="update",
        )(
            table[current],
            *[in_hbm(part) for part in newest],
            *before,
            *[in_hbm(chunks[k]) for k in used],
        )
        return result[0], history + list(result[1:])

    split = rhs.reshape(blocks, height, members, columns).transpose(2, 0, 1, 3)
    split = lax.all_to_all(split, (ROWS, CORES), 0, 0, tiled=True)
    gather_chunk(0, None)
    copies = first(split)
    block_index, copies = lax.optimization_barrier((block_index, copies))
    block_rows, block_cols = block_index[:, 0], block_index[:, 1]
    numbers = jnp.arange(blocks, dtype=jnp.int32)
    match = (block_rows[None, None, :] == numbers[:, None, None]) & (
        block_cols[None, None, :] == numbers[None, :, None]
    )
    places = jnp.arange(1, entries + 1, dtype=jnp.int32)
    table = jnp.sum(jnp.where(match, places, 0), axis=2) - 1

    gather_chunk(1, None)
    picked = pick(0)
    pieces = earlier = None
    history = []
    starts = {first_row: number for number, (first_row, _) in enumerate(CHUNK_ROWS)}
    for current in range(blocks):
        last = current + 1 == blocks
        gathered = exchange(copies)
        for number, after in enumerate(CHUNK_AFTER):
            if after == current:
                gather_chunk(number, gathered)
        copies, pieces = solve(current, gathered, picked, pieces)
        if last:
            break
        if current == 0:
            table, copies = lax.optimization_barrier((table, copies))
        if current == 1:
            chunks[1], copies = lax.optimization_barrier((chunks[1], copies))
        picked = pick(current + 1)
        gathered = exchange(copies)
        copies, *kept = residual(current + 1, gathered, picked, split, earlier)
        number = starts.get(current + 2)
        if number is not None and number > 1:
            chunks[number], copies = lax.optimization_barrier((chunks[number], copies))
        if current + 2 < blocks:
            sums, history = update(current + 2, (kept[0], other_core(kept[0])), history)
            earlier = sums, other_core(sums[1])

    out = lax.all_to_all(pieces, (ROWS, CORES), 0, 0, tiled=True)
    return out.transpose(1, 2, 0, 3).reshape(blocks, height, total_columns)


def solution(mesh):
    cores = 2
    across, along = mesh.shape["prow"], mesh.shape["pcol"]
    grid = Mesh(mesh.devices.reshape(across, along // cores, cores), (ROWS, CHIPS, CORES))
    column = (CHIPS, CORES)
    in_specs = (
        P(None, (ROWS, CHIPS, CORES), None),
        P(None, None, column, None, ROWS),
        P(None, None, column, None, ROWS),
        P(),
    )
    out_specs = P(None, (ROWS, CHIPS, CORES), None)
    return jax.shard_map(shards, mesh=grid, in_specs=in_specs, out_specs=out_specs, check_vma=False)
```

```python
import jax
import jax.numpy as jnp
from jax import lax
from jax.experimental import pallas as pl
from jax.experimental.pallas import tpu as pltpu
from jax.sharding import Mesh, PartitionSpec as P

ROWS, CHIPS, CORES = "prow", "chip", "core"
LANES = 128
CHUNK_ROWS = ((0, 1), (2, 3), (4, 5), (6, 7), (8, 8), (9, 11))
CHUNK_AFTER = (None, None, 0, 2, 4, 5)


def exchange(copies):
    return lax.all_to_all(copies, CHIPS, 0, 0, tiled=True)


def other_core(array):
    return lax.ppermute(array, CORES, [(0, 1), (1, 0)])


def lane_of(shape):
    return lax.broadcasted_iota(jnp.int32, shape, 1)


def pack(value):
    lane = lane_of((16, LANES))

    def tile(core, part):
        first = (core * 4 + part) * 16
        return value[first : first + 16]

    def head(core):
        return jnp.where(
            lane < 48,
            tile(core, 0),
            jnp.where(lane < 96, pltpu.roll(tile(core, 1), 48, 1), pltpu.roll(tile(core, 2), 96, 1)),
        )

    low = jnp.where(lane < 16, pltpu.roll(tile(0, 2), 96, 1), pltpu.roll(tile(0, 3), 16, 1))
    high = jnp.where(lane < 80, pltpu.roll(tile(1, 2), 32, 1), pltpu.roll(tile(1, 3), 80, 1))
    tail = jnp.where(lane < 64, low, high)
    return jnp.concatenate([head(0), head(1), tail], axis=0).astype(jnp.bfloat16)


def unpack(gathered, whole, unroll=32):
    def place(chip, carry):
        first = pl.multiple_of(chip * 32, 32)
        whole[pl.ds(first, 32), pl.ds(0, LANES)] = gathered[chip, pl.ds(0, 32), :]
        tail = gathered[chip, pl.ds(32, 16), :]
        moved = pltpu.roll(tail.astype(jnp.float32), 64, 1).astype(jnp.bfloat16)
        whole[pl.ds(first, 16), pl.ds(LANES, LANES)] = tail
        whole[pl.ds(first + 16, 16), pl.ds(LANES, LANES)] = moved
        return carry

    lax.fori_loop(0, gathered.shape[0], place, 0, unroll=unroll)


def unpack_both(own, other, whole):
    low = lane_of((16, LANES)) < 64

    def place(chip, carry):
        first = pl.multiple_of(chip * 32, 32)
        whole[pl.ds(first, 32), pl.ds(0, LANES)] = own[chip, pl.ds(0, 32), :]
        whole[pl.ds(first, 32), pl.ds(LANES, LANES)] = other[chip, pl.ds(0, 32), :]
        one = own[chip, pl.ds(32, 16), :].astype(jnp.float32)
        two = other[chip, pl.ds(32, 16), :].astype(jnp.float32)
        tails = jnp.where(low, one, pltpu.roll(two, 64, 1))
        whole[pl.ds(first, 16), pl.ds(2 * LANES, LANES)] = tails.astype(jnp.bfloat16)
        tails = jnp.where(low, pltpu.roll(one, 64, 1), two)
        whole[pl.ds(first + 16, 16), pl.ds(2 * LANES, LANES)] = tails.astype(jnp.bfloat16)
        return carry

    lax.fori_loop(0, own.shape[0], place, 0, unroll=8)


def combine(raw, rows, head=0, tail=LANES, shift=0):
    def of(part, lanes):
        return raw[part * rows : (part + 1) * rows, lanes : lanes + LANES]

    def moved(value, by):
        return pltpu.roll(value, by % LANES, 1)

    second = jnp.where(
        lane_of((rows, LANES)) < 32, moved(of(2, head), 32), moved(of(2, tail), 32 - shift)
    )
    first = of(0, head) + moved(of(1, head), 80)
    return first + (second + moved(of(3, tail), 112 - shift))


def chain_product(own, other, which, whole):
    _, parts, rows, _ = own.shape
    stacked = jnp.concatenate(
        [matrices[which, part] for part in range(parts) for matrices in (own, other)], axis=0
    )
    raw = jnp.dot(stacked, whole[...], preferred_element_type=jnp.float32)
    return combine(raw, 2 * rows)


def core_rows(rows):
    core = lax.axis_index(CORES)
    return (
        pl.ds(pl.multiple_of(core * rows, rows), rows),
        pl.ds(pl.multiple_of((1 - core) * rows, rows), rows),
    )


def copy_out(value, packed, copies, sem):
    packed[...] = value
    for chip in range(copies.shape[0]):
        pltpu.make_async_copy(packed, copies.at[chip], sem).start()
    pltpu.make_async_copy(copies, copies, sem).wait()


def widen(rhs, wide):
    members, height, columns = rhs.shape
    wide[...] = jnp.zeros_like(wide)
    for member in range(members):
        part, core = member // 2, member % 2
        wide[pl.ds((core * 4 + part) * height, height), pl.ds(0, columns)] = rhs[
            member
        ].astype(jnp.float32)


def start_entry(entry, chunks, spans, target, sem):
    for chunk, (low, high, offset) in zip(chunks, spans):

        @pl.when((entry >= low) & (entry < high))
        def _(chunk=chunk, low=low, high=high, offset=offset):
            place = jnp.clip(entry - low, 0, high - low - 1) + offset
            pltpu.make_async_copy(chunk.at[:, place], target, sem).start()


def wait_entry(chunks, target, sem):
    pltpu.make_async_copy(chunks[0].at[:, 0], target, sem).wait()


def first_kernel(rhs, copies, wide, packed, sem):
    widen(rhs[:, 0], wide)
    copy_out(pack(wide[...]), packed, copies, sem)


def pick_kernel(current, place, spans, own, *refs):
    if current:
        slots, refs = refs[0], refs[1:]
    chunks, (blocks, sems) = refs[: len(spans)], refs[len(spans) :]
    load = pltpu.make_async_copy(own.at[:, place], blocks.at[0], sems.at[0])
    load.start()
    if current:
        entry = slots[current - 1]
        start_entry(entry, chunks, spans, blocks.at[1], sems.at[1])

        @pl.when(entry < 0)
        def _():
            blocks[1] = jnp.zeros_like(blocks[1])

        @pl.when(entry >= 0)
        def _():
            wait_entry(chunks, blocks.at[1], sems.at[1])

    load.wait()


def hold_kernel(there, here, sem):
    load = pltpu.make_async_copy(there, here, sem)
    load.start()
    load.wait()


def solve_kernel(current, gathered, own, other, *refs):
    if current:
        refs = refs[1:]
    copies, pieces, whole, total, packed, sem, piece, piece_sem = refs
    members, blocks, height, columns = pieces.shape
    rows = own.shape[2]
    unpack(gathered, whole)
    value = chain_product(own, other, 0, whole)
    for number, place in enumerate(core_rows(rows)):
        total[place, :] = value[number * rows : (number + 1) * rows]
    value = total[...]
    rounded = value[:, :columns].astype(jnp.bfloat16)
    for member in range(members):
        first = (member % 2 * 4 + member // 2) * height
        piece[member] = rounded[first : first + height]
    keep = pltpu.make_async_copy(piece, pieces.at[:, current], piece_sem)
    keep.start()
    if current + 1 < blocks:
        copy_out(pack(value), packed, copies, sem)
    keep.wait()


def residual_kernel(current, gathered, own, other, rhs, *refs):
    if current > 1:
        sums, others, refs = refs[0], refs[1], refs[2:]
    copies, refs = refs[0], refs[1:]
    keeps = current + 1 < rhs.shape[1]
    if keeps:
        kept, refs = refs[0], refs[1:]
    whole, total, packed, sem, piece, piece_sem, earlier, sems, keep_sem = refs
    loads = [pltpu.make_async_copy(rhs.at[:, current], piece, piece_sem)]
    if current > 1:
        for core, array in enumerate((sums.at[0], others)):
            loads.append(pltpu.make_async_copy(array, earlier.at[core], sems.at[core]))
    for load in loads:
        load.start()
    rows = own.shape[2]
    places = core_rows(rows)
    if keeps:
        keep = pltpu.make_async_copy(gathered, kept, keep_sem)
        keep.start()
    unpack(gathered, whole, 8 if keeps else 32)
    value = chain_product(own, other, 1, whole)
    for load in loads:
        load.wait()
    widen(piece, total)
    if current > 1:
        for core, place in enumerate(places):
            total[place, :] -= earlier[core]
    for number, place in enumerate(places):
        total[place, :] -= value[number * rows : (number + 1) * rows]

    copy_out(pack(total[...]), packed, copies, sem)
    if keeps:
        keep.wait()


def update_kernel(spans, keeps, slots, own, other, *refs):
    result, refs_in, refs = refs[-9 - keeps], refs[: -9 - keeps], refs[-8 - keeps :]
    history, chunks = refs_in[: -len(spans)], refs_in[-len(spans) :]
    if keeps:
        kept, refs = refs[0], refs[1:]
    wholes, matrices, total, received, summed, sems, factor_sems, received_sems = refs
    count, parts, rows, span = matrices.shape
    newest = count - 1
    arrivals = [
        pltpu.make_async_copy(array, received.at[core], received_sems.at[core])
        for core, array in enumerate((own, other))
    ]
    for arrival in arrivals:
        arrival.start()

    def start_factor(column, carry):
        start_entry(slots[column], chunks, spans, matrices.at[column], factor_sems.at[column])
        return carry

    lax.fori_loop(0, count, start_factor, 0)
    for column in range(newest):

        @pl.when(slots[column] >= 0)
        def _(column=column):
            pltpu.make_async_copy(history[column], wholes.at[column], sems.at[column]).start()

    for arrival in arrivals:
        arrival.wait()
    unpack_both(received.at[0], received.at[1], wholes.at[newest])
    if keeps:
        keep = pltpu.make_async_copy(wholes.at[newest], kept, sems.at[newest])
        keep.start()
    total[...] = jnp.zeros_like(total)

    def add(column):
        wait_entry(chunks, matrices.at[column], factor_sems.at[column])
        total[...] += jnp.dot(
            matrices[column].reshape(parts * rows, span),
            wholes[column],
            preferred_element_type=jnp.float32,
        )

    def add_earlier(column, carry):
        @pl.when(slots[column] >= 0)
        def _():
            pltpu.make_async_copy(history[0], wholes.at[column], sems.at[column]).wait()
            add(column)

        return carry

    if newest:
        lax.fori_loop(0, newest, add_earlier, 0)

    @pl.when(slots[newest] >= 0)
    def _():
        add(newest)

    raw = total[...]
    for core in range(2):
        summed[core] = combine(raw, rows, core * LANES, 2 * LANES, core * 64)
    store = pltpu.make_async_copy(summed, result, received_sems.at[0])
    store.start()
    store.wait()
    if keeps:
        keep.wait()


def vmem():
    return pl.BlockSpec(memory_space=pltpu.VMEM)


def smem():
    return pl.BlockSpec(memory_space=pltpu.SMEM)


def anywhere():
    return pl.BlockSpec(memory_space=pl.ANY)


def in_vmem(array):
    return pltpu.with_memory_space_constraint(array, pltpu.VMEM)


def in_hbm(array):
    return pltpu.with_memory_space_constraint(array, pltpu.HBM)


LIMIT = pltpu.CompilerParams(vmem_limit_bytes=24 * 1024 * 1024)


def shards(rhs, factor_blocks, diag_inverses, block_index):
    blocks, height, total_columns = rhs.shape
    entries, parts = factor_blocks.shape[:2]
    span = factor_blocks.shape[-1]
    cores = 2
    members = parts * cores
    rows = parts * height
    columns = total_columns // members
    chips = span // (height * cores)
    factor = factor_blocks.reshape(entries, rows, span)
    inverse = diag_inverses.reshape(blocks, rows, span)
    copies_shape = pltpu.HBM((chips, 48, LANES), jnp.bfloat16)
    copy_scratch = [pltpu.VMEM((48, LANES), jnp.bfloat16), pltpu.SemaphoreType.DMA]
    piece_scratch = [
        pltpu.VMEM((members, height, columns), jnp.bfloat16),
        pltpu.SemaphoreType.DMA,
    ]
    pieces_shape = pltpu.HBM((members, blocks, height, columns), jnp.bfloat16)
    history_shape = pltpu.HBM((span, 3 * LANES), jnp.bfloat16)
    sums_shape = pltpu.HBM((cores, rows, LANES), jnp.float32)
    whole_scratch = pltpu.VMEM((span, 2 * LANES), jnp.bfloat16)
    wide_scratch = pltpu.VMEM((cores * rows, LANES), jnp.float32)

    def most(last):
        return min(entries, last * (last + 1) // 2)

    bounds = [0] + [most(last) for _, last in CHUNK_ROWS]
    sizes = [last + 1 - first for first, last in CHUNK_ROWS]
    spans = [(low, high, size) for low, high, size in zip(bounds, bounds[1:], sizes)]
    chunks = [None] * len(spans)

    def gather_chunk(number, after):
        first, last = CHUNK_ROWS[number]
        low, high, _ = spans[number]
        slab = jnp.concatenate([inverse[first : last + 1], factor[low:high]], axis=0)
        if after is not None:
            slab, after = lax.optimization_barrier((slab, after))
        chunks[number] = lax.all_gather(slab, ROWS, axis=0)

    def chunks_of(current):
        high = most(current)
        low = max(0, entries - sum(range(current, blocks)))
        return [k for k, (a, b, _) in enumerate(spans) if a < high and b > low]

    def first(split):
        return pl.pallas_call(
            first_kernel,
            out_shape=copies_shape,
            in_specs=[vmem()],
            out_specs=anywhere(),
            scratch_shapes=[wide_scratch, *copy_scratch],
            compiler_params=LIMIT,
            name="first",
        )(in_vmem(split))

    def pick(current):
        number = next(k for k, (a, b) in enumerate(CHUNK_ROWS) if a <= current <= b)
        place = current - CHUNK_ROWS[number][0]
        used = chunks_of(current) if current else []
        kinds = 2 if current else 1
        used_rows = [current] if current else []
        picked = pl.pallas_call(
            lambda *refs: pick_kernel(current, place, [spans[k] for k in used], *refs),
            out_shape=pltpu.VMEM((kinds, parts, rows, span), jnp.bfloat16),
            in_specs=[anywhere(), smem()][:kinds] + [anywhere()] * len(used),
            out_specs=vmem(),
            scratch_shapes=[pltpu.SemaphoreType.DMA((2,))],
            compiler_params=LIMIT,
            cost_estimate=pl.CostEstimate(
                flops=0, bytes_accessed=2 * kinds * parts * rows * span * 2, transcendentals=0
            ),
            name="pick",
        )(
            in_hbm(chunks[number]), *[table[k] for k in used_rows], *[in_hbm(chunks[k]) for k in used]
        )
        return picked, hold(other_core(picked))

    def hold(array):
        return pl.pallas_call(
            hold_kernel,
            out_shape=pltpu.VMEM(array.shape, array.dtype),
            in_specs=[anywhere()],
            out_specs=vmem(),
            scratch_shapes=[pltpu.SemaphoreType.DMA],
            compiler_params=LIMIT,
            cost_estimate=pl.CostEstimate(
                flops=0, bytes_accessed=4 * array.size, transcendentals=0
            ),
            name="hold",
        )(array)

    def solve(current, gathered, picked, pieces):
        operands = [in_vmem(array) for array in (gathered, *picked)]
        if current:
            operands.append(in_hbm(pieces))
        return pl.pallas_call(
            lambda *refs: solve_kernel(current, *refs),
            out_shape=(copies_shape, pieces_shape),
            in_specs=[vmem(), vmem(), vmem(), anywhere()][: len(operands)],
            out_specs=(anywhere(), anywhere()),
            input_output_aliases={3: 1} if current else {},
            scratch_shapes=[whole_scratch, wide_scratch, *copy_scratch, *piece_scratch],
            compiler_params=LIMIT,
            name="solve",
        )(*operands)

    def residual(current, gathered, picked, split, earlier):
        held = [in_vmem(array) for array in (gathered, *picked)]
        operands = [in_hbm(split)]
        if current > 1:
            operands += [in_hbm(array) for array in earlier]
        outputs = 2 if current + 1 < blocks else 1
        return pl.pallas_call(
            lambda *refs: residual_kernel(current, *refs),
            out_shape=(copies_shape,) * outputs,
            in_specs=[vmem()] * 3 + [anywhere()] * len(operands),
            out_specs=(anywhere(),) * outputs,
            scratch_shapes=[
                whole_scratch,
                wide_scratch,
                *copy_scratch,
                *piece_scratch,
                pltpu.VMEM((cores, rows, LANES), jnp.float32),
                pltpu.SemaphoreType.DMA((2,)),
                pltpu.SemaphoreType.DMA,
            ],
            compiler_params=LIMIT,
            name="residual",
        )(*held, *operands)

    def update(current, newest, history):
        used = chunks_of(current)
        count = current - 1
        keeps = current + 1 < blocks
        before = [in_hbm(array) for array in history]
        result = pl.pallas_call(
            lambda *refs: update_kernel([spans[k] for k in used], keeps, *refs),
            out_shape=(sums_shape, history_shape) if keeps else (sums_shape,),
            in_specs=[smem()] + [anywhere()] * (2 + len(before) + len(used)),
            out_specs=(anywhere(),) * (1 + keeps),
            scratch_shapes=[
                pltpu.VMEM((count, span, 3 * LANES), jnp.bfloat16),
                pltpu.VMEM((count, parts, rows, span), jnp.bfloat16),
                pltpu.VMEM((parts * rows, 3 * LANES), jnp.float32),
                pltpu.VMEM((cores, chips, 48, LANES), jnp.bfloat16),
                pltpu.VMEM((cores, rows, LANES), jnp.float32),
                pltpu.SemaphoreType.DMA((count,)),
                pltpu.SemaphoreType.DMA((count,)),
                pltpu.SemaphoreType.DMA((2,)),
            ],
            compiler_params=LIMIT,
            cost_estimate=pl.CostEstimate(
                flops=count * 2 * cores * parts * rows * span * 256,
                bytes_accessed=count * parts * span * (rows + LANES) * 2,
                transcendentals=0,
            ),
            name="update",
        )(
            table[current],
            *[in_hbm(part) for part in newest],
            *before,
            *[in_hbm(chunks[k]) for k in used],
        )
        return result[0], history + list(result[1:])

    split = rhs.reshape(blocks, height, members, columns).transpose(2, 0, 1, 3)
    split = lax.all_to_all(split, (ROWS, CORES), 0, 0, tiled=True)
    gather_chunk(0, None)
    copies = first(split)
    block_index, inverse, factor, copies = lax.optimization_barrier(
        (block_index, inverse, factor, copies)
    )
    block_rows, block_cols = block_index[:, 0], block_index[:, 1]
    numbers = jnp.arange(blocks, dtype=jnp.int32)
    match = (block_rows[None, None, :] == numbers[:, None, None]) & (
        block_cols[None, None, :] == numbers[None, :, None]
    )
    places = jnp.arange(1, entries + 1, dtype=jnp.int32)
    table = jnp.sum(jnp.where(match, places, 0), axis=2) - 1

    gather_chunk(1, None)
    picked = pick(0)
    pieces = earlier = None
    history = []
    starts = {first_row: number for number, (first_row, _) in enumerate(CHUNK_ROWS)}
    for current in range(blocks):
        last = current + 1 == blocks
        gathered = exchange(copies)
        for number, after in enumerate(CHUNK_AFTER):
            if after == current:
                gather_chunk(number, gathered)
        copies, pieces = solve(current, gathered, picked, pieces)
        if last:
            break
        if current == 0:
            table, copies = lax.optimization_barrier((table, copies))
        if current == 1:
            chunks[1], copies = lax.optimization_barrier((chunks[1], copies))
        picked = pick(current + 1)
        gathered = exchange(copies)
        copies, *kept = residual(current + 1, gathered, picked, split, earlier)
        number = starts.get(current + 2)
        if number is not None and number > 1:
            chunks[number], copies = lax.optimization_barrier((chunks[number], copies))
        if current + 2 < blocks:
            sums, history = update(current + 2, (kept[0], other_core(kept[0])), history)
            earlier = sums, other_core(sums[1])

    out = lax.all_to_all(pieces, (ROWS, CORES), 0, 0, tiled=True)
    return out.transpose(1, 2, 0, 3).reshape(blocks, height, total_columns)


def solution(mesh):
    cores = 2
    across, along = mesh.shape["prow"], mesh.shape["pcol"]
    grid = Mesh(mesh.devices.reshape(across, along // cores, cores), (ROWS, CHIPS, CORES))
    column = (CHIPS, CORES)
    in_specs = (
        P(None, (ROWS, CHIPS, CORES), None),
        P(None, None, column, None, ROWS),
        P(None, None, column, None, ROWS),
        P(),
    )
    out_specs = P(None, (ROWS, CHIPS, CORES), None)
    return jax.shard_map(shards, mesh=grid, in_specs=in_specs, out_specs=out_specs, check_vma=False)
```
